32 devices in a mesh: ctx: 4 (over y, x), fsdp: 8 (over z, core).
Axes of the slice: x: 2, y: 2, z: 4, core: 2. Of those that a mesh axis runs over, the one named last changes fastest.
Arguments:
- tokens: bfloat16 [8, 4, 2, 256, 1024], P('fsdp', 'ctx'), may hold values from -6 to 6
- cotangent: bfloat16 [8, 4, 2, 256, 1024], P('fsdp', 'ctx'), may hold values from -6 to 6
- block_pair: int32 [4], replicated, may hold values from 0 to 3, each once
- segment_ids: int32 [8, 2048], P('fsdp'), may hold values from 0 to 2, as said below
- attn_gain: float32 [1024], replicated, may hold values from 0.5 to 1.5
- query_gain: float32 [64], replicated, may hold values from 0.5 to 1.5
- key_gain: float32 [64], replicated, may hold values from 0.5 to 1.5
- ffn_gain: float32 [1024], replicated, may hold values from 0.5 to 1.5
- w_query: bfloat16 [1024, 1024], P('fsdp'), may hold values from -0.1875 to 0.1875
- w_key: bfloat16 [1024, 512], P('fsdp'), may hold values from -0.1875 to 0.1875
- w_value: bfloat16 [1024, 512], P('fsdp'), may hold values from -0.1875 to 0.1875
- w_output: bfloat16 [1024, 1024], P('fsdp'), may hold values from -4 to 4
- w_gate: bfloat16 [1024, 4608], P('fsdp'), may hold values from -0.1875 to 0.1875
- w_up: bfloat16 [1024, 4608], P('fsdp'), may hold values from -0.1875 to 0.1875
- w_down: bfloat16 [4608, 1024], P('fsdp'), may hold values from -0.09375 to 0.09375
Outputs:
- output: bfloat16 [8, 4, 2, 256, 1024], P('fsdp', 'ctx')
- input_grad: float32 [8, 4, 2, 256, 1024], P('fsdp', 'ctx')
- attn_gain_grad: float32 [1024], P(('ctx', 'fsdp'))
- query_gain_grad: float32 [64], replicated
- key_gain_grad: float32 [64], replicated
- ffn_gain_grad: float32 [1024], P(('ctx', 'fsdp'))
- w_query_grad: float32 [1024, 1024], P(('ctx', 'fsdp'))
- w_key_grad: float32 [1024, 512], P(('ctx', 'fsdp'))
- w_value_grad: float32 [1024, 512], P(('ctx', 'fsdp'))
- w_output_grad: float32 [1024, 1024], P(('ctx', 'fsdp'))
- w_gate_grad: float32 [1024, 4608], P(('ctx', 'fsdp'))
- w_up_grad: float32 [1024, 4608], P(('ctx', 'fsdp'))
- w_down_grad: float32 [4608, 1024], P(('ctx', 'fsdp'))
The draws below stay inside these ranges and needn't reach their ends.
Inputs may be any that keep to these rules, and one draw needn't show every extreme that they name: `block_pair`: each ctx index holds a different pair of blocks. `segment_ids`: never falling along a sequence; document 0 starts each sequence and covers at least its first 1024 positions.
All inputs are finite; a program needn't handle non-finite values.
Results may differ from the reference program's by a relative error of at most 0.023.
Values may be sent and summed in bfloat16 or wider, within the bound.
A program may use at most 192 MiB of HBM per device.

```python
import math
import jax
import jax.numpy as jnp
from jax import lax

D = 1024
FF = 4608
Q_HEADS = 16
KV_HEADS = 8
HEAD_DIM = 64
BLK = 256
SEQS = 8
LEN = 2048
N_CTX = 4


def draw_segment_ids(key, part):
    key = jax.random.fold_in(key, 7)
    first_key, second_key = jax.random.split(key)
    first_cut = jax.random.randint(first_key, (SEQS, 1), LEN // 2, 3 * LEN // 4 + 1)
    second_cut = jax.random.randint(second_key, (SEQS, 1), first_cut + 1, LEN)
    places = jnp.arange(LEN, dtype=jnp.int32)[None, :]
    return (places >= first_cut).astype(jnp.int32) + (places >= second_cut).astype(jnp.int32)


def shard_levels(own_key, shape, cuts, least, top_value):
    factor_of, own = 1.0, jax.random.fold_in(own_key, 6)
    for dim, parts in cuts:
        steps = jnp.exp(jax.random.uniform(jax.random.fold_in(own, dim), (parts,), jnp.float32, least / len(cuts), top_value / len(cuts)))
        factor_of = factor_of * jnp.repeat(steps, shape[dim] // parts).reshape([-1 if axis == dim else 1 for axis in range(len(shape))])
    return factor_of


def bell_draw(key, extent, scale, limit, cuts=(), kind=jnp.bfloat16):
    values = scale * jax.random.normal(key, extent, jnp.float32)
    if cuts:
        values = values * shard_levels(key, extent, cuts, -0.22, 0.18)
    return jnp.clip(values, -limit, limit).astype(kind)


def setup_inputs(seed: int = 0) -> dict:
    arg_keys = jax.random.split(jax.random.key(seed), 16)
    tokens = bell_draw(arg_keys[0], (SEQS, N_CTX, 2, BLK, D), 1.0, 6.0, ((0, 8), (1, 4)))
    cotangent = bell_draw(arg_keys[1], (SEQS, N_CTX, 2, BLK, D), 1.0, 6.0, ((0, 8), (1, 4)))
    block_pair = jax.random.permutation(arg_keys[2], N_CTX).astype(jnp.int32)
    segment_ids = draw_segment_ids(jax.random.fold_in(arg_keys[15], 71), 0)
    attn_gain = jnp.clip(1.0 + 0.1 * jax.random.normal(arg_keys[4], (D,), jnp.float32), 0.5, 1.5)
    query_gain = jnp.clip(1.0 + 0.1 * jax.random.normal(arg_keys[5], (HEAD_DIM,), jnp.float32), 0.5, 1.5)
    key_gain = jnp.clip(1.0 + 0.1 * jax.random.normal(arg_keys[6], (HEAD_DIM,), jnp.float32), 0.5, 1.5)
    ffn_gain = jnp.clip(1.0 + 0.1 * jax.random.normal(arg_keys[7], (D,), jnp.float32), 0.5, 1.5)
    w_query = bell_draw(arg_keys[8], (D, Q_HEADS * HEAD_DIM), D ** -0.5, 0.1875, ((0, 8),))
    w_key = bell_draw(arg_keys[9], (D, KV_HEADS * HEAD_DIM), D ** -0.5, 0.1875, ((0, 8),))
    w_value = bell_draw(arg_keys[10], (D, KV_HEADS * HEAD_DIM), D ** -0.5, 0.1875, ((0, 8),))
    w_output = bell_draw(arg_keys[11], (Q_HEADS * HEAD_DIM, D), (max(1, 4 * Q_HEADS * HEAD_DIM // (2 * N_CTX * BLK))) ** -0.5, 4.0, ((0, 8),))
    w_gate = bell_draw(arg_keys[12], (D, FF), D ** -0.5, 0.1875, ((0, 8),))
    w_up = bell_draw(arg_keys[13], (D, FF), D ** -0.5, 0.1875, ((0, 8),))
    w_down = bell_draw(arg_keys[14], (FF, D), FF ** -0.5, 0.09375, ((0, 8),))
    return {"tokens": tokens, "cotangent": cotangent, "block_pair": block_pair, "segment_ids": segment_ids, "attn_gain": attn_gain, "query_gain": query_gain, "key_gain": key_gain, "ffn_gain": ffn_gain, "w_query": w_query, "w_key": w_key, "w_value": w_value, "w_output": w_output, "w_gate": w_gate, "w_up": w_up, "w_down": w_down}


@jax.custom_vjp
def low(v):
    return lax.optimization_barrier(v.astype(jnp.bfloat16)).astype(jnp.float32)

@jax.custom_vjp
def low_back(v):
    return v

def low_keep(v):
    return (low(v), None)

def low_pass(kept, grad):
    return (grad,)

def back_keep(v):
    return (v, None)

def back_low(kept, grad):
    return (low(grad),)
low.defvjp(low_keep, low_pass)
low_back.defvjp(back_keep, back_low)
EPSILON = 1e-05
ROPE_THETA = 1000000.0
MASKED_SCORE = -1e+30
HIGHEST = lax.Precision.HIGHEST

def norm_rows(value, gain):
    return value * lax.rsqrt(lax.optimization_barrier(jnp.mean(value * value, axis=-1, keepdims=True)) + EPSILON) * gain

def turn_half(value):
    middle = value.shape[-1] // 2
    return jnp.concatenate([-value[..., middle:], value[..., :middle]], axis=-1)

def angles(positions, head_size):
    middle = head_size // 2
    freqs = ROPE_THETA ** (-jnp.arange(middle, dtype=jnp.float32) * 2.0 / head_size)
    phase = positions.astype(jnp.float32)[:, None] * freqs[None, :]
    phase = jnp.concatenate([phase, phase], axis=-1)
    return (jnp.cos(phase)[:, None, :], jnp.sin(phase)[:, None, :])

def block_forward(seq_inputs, w_query, w_key, w_value, w_output, w_gate, w_up, w_down, attn_gain, query_gain, key_gain, ffn_gain, cosine, sine_part, positions, seg_rows):
    total_rows = seq_inputs.shape[0]
    group_size = Q_HEADS // KV_HEADS
    score_scale = HEAD_DIM ** (-0.5)
    attn_in = low(norm_rows(seq_inputs, attn_gain))
    query_raw = low_back(jnp.dot(attn_in, w_query, precision=HIGHEST)).reshape(total_rows, Q_HEADS, HEAD_DIM)
    key_raw = low_back(jnp.dot(attn_in, w_key, precision=HIGHEST)).reshape(total_rows, KV_HEADS, HEAD_DIM)
    values = low(low_back(jnp.dot(attn_in, w_value, precision=HIGHEST))).reshape(total_rows, KV_HEADS, HEAD_DIM)
    query_normed = norm_rows(query_raw, query_gain)
    key_normed = norm_rows(key_raw, key_gain)
    queries = low(query_normed * cosine + turn_half(query_normed) * sine_part)
    keys_all = low(key_normed * cosine + turn_half(key_normed) * sine_part)
    queries = queries.reshape(total_rows, KV_HEADS, group_size, HEAD_DIM)
    block_rows = math.gcd(total_rows, 512)
    block_count = total_rows // block_rows

    def attend(item):
        query_block, query_pos, query_seg = item
        raw_scores = jnp.einsum('qhgd,khd->qhgk', query_block, keys_all, precision=HIGHEST) * score_scale
        scores = low_back(raw_scores)
        allowed = (positions[None, :] <= query_pos[:, None]) & (seg_rows[None, :] == query_seg[:, None])
        allowed = allowed[:, None, None, :]
        masked = jnp.where(allowed, scores, MASKED_SCORE)
        peak = lax.optimization_barrier(jnp.max(masked, axis=-1, keepdims=True))
        weights_raw = jnp.where(allowed, jnp.exp(masked - peak), 0.0)
        attn_probs = low(weights_raw / lax.optimization_barrier(jnp.sum(weights_raw, axis=-1, keepdims=True)))
        return jnp.einsum('qhgk,khd->qhgd', attn_probs, values, precision=HIGHEST)
    mixed = lax.map(jax.checkpoint(attend), (queries.reshape(block_count, block_rows, KV_HEADS, group_size, HEAD_DIM), positions.reshape(block_count, block_rows), seg_rows.reshape(block_count, block_rows)))
    mixed = low(low_back(mixed.reshape(total_rows, Q_HEADS * HEAD_DIM)))
    residual = seq_inputs + low_back(jnp.dot(mixed, w_output, precision=HIGHEST))
    ffn_in = low(norm_rows(residual, ffn_gain))
    gate = low_back(jnp.dot(ffn_in, w_gate, precision=HIGHEST))
    upward = low_back(jnp.dot(ffn_in, w_up, precision=HIGHEST))
    activation = low(jax.nn.silu(gate) * upward)
    return residual + low_back(jnp.dot(activation, w_down, precision=HIGHEST))

def reference(tokens, cotangent, block_pair, segment_ids, attn_gain, query_gain, key_gain, ffn_gain, w_query, w_key, w_value, w_output, w_gate, w_up, w_down):
    ctx_count = tokens.shape[1]
    block_len = tokens.shape[3]
    model_width = tokens.shape[4]
    total_rows = 2 * ctx_count * block_len
    blocks = jnp.stack([block_pair, 2 * ctx_count - 1 - block_pair], axis=1).reshape(-1).astype(jnp.int32)
    positions = (blocks[:, None] * block_len + jnp.arange(block_len, dtype=jnp.int32)[None, :]).reshape(-1)
    cosine, sine_part = angles(positions, HEAD_DIM)
    params = tuple((item.astype(jnp.float32) for item in (w_query, w_key, w_value, w_output, w_gate, w_up, w_down, attn_gain, query_gain, key_gain, ffn_gain)))

    def one_sequence(totals, item):
        seq_inputs, seq_grad, seq_segments = item
        seg_rows = jnp.take(seq_segments.reshape(2 * ctx_count, block_len), blocks, axis=0).reshape(-1)

        def forward(inputs_now, *weights):
            return block_forward(inputs_now, *weights, cosine, sine_part, positions, seg_rows)
        result, pullback = jax.vjp(forward, seq_inputs.reshape(total_rows, model_width).astype(jnp.float32), *params)
        gradients = pullback(seq_grad.reshape(total_rows, model_width).astype(jnp.float32))
        totals = tuple((before + after for before, after in zip(totals, gradients[1:])))
        return (totals, (result.astype(jnp.bfloat16), gradients[0]))
    zeros_start = tuple((jnp.zeros_like(item) for item in params))
    totals, (results, input_grads) = lax.scan(one_sequence, zeros_start, (tokens, cotangent, segment_ids))
    return (results.reshape(tokens.shape), input_grads.reshape(tokens.shape), totals[7], totals[8], totals[9], totals[10], totals[0], totals[1], totals[2], totals[3], totals[4], totals[5], totals[6])
```

```python
import math

import jax
import jax.numpy as jnp
from jax import lax
from jax.sharding import PartitionSpec as P

Q_HEADS = 16
KV_HEADS = 8
HEAD_DIM = 64


EPSILON = 1e-05
ROPE_THETA = 1000000.0
MASKED_SCORE = -1e30


def norm_parts(value, gain):
    factor = lax.rsqrt(jnp.mean(value * value, axis=-1, keepdims=True) + EPSILON)
    normal = value * factor
    return (normal * gain, normal, factor)


def norm_back(grad_in, normal, factor, gain):
    inner = grad_in * gain
    back = factor * (inner - normal * jnp.mean(inner * normal, axis=-1, keepdims=True))
    return (back, grad_in * normal)


def turn_half(value):
    middle = value.shape[-1] // 2
    return jnp.concatenate([-value[..., middle:], value[..., :middle]], axis=-1)


def turn_back(value):
    middle = value.shape[-1] // 2
    return jnp.concatenate([value[..., middle:], -value[..., :middle]], axis=-1)


def angles(positions, head_size):
    middle = head_size // 2
    freqs = ROPE_THETA ** (-jnp.arange(middle, dtype=jnp.float32) * 2.0 / head_size)
    phase = positions.astype(jnp.float32)[:, None] * freqs[None, :]
    phase = jnp.concatenate([phase, phase], axis=-1)
    return (jnp.cos(phase)[:, None, :], jnp.sin(phase)[:, None, :])


def contract_rows(left, right):
    return lax.dot_general(
        left, right, (((0,), (0,)), ((), ())), preferred_element_type=jnp.float32
    )


def times_transposed(left, right):
    return lax.dot_general(
        left, right, (((1,), (1,)), ((), ())), preferred_element_type=jnp.float32
    )


def bit_count(size):
    return size.bit_length() - 1


def swap(value, axis_name, bit):
    size = lax.axis_size(axis_name)
    return lax.ppermute(value, axis_name, [(i, i ^ (1 << bit)) for i in range(size)])


def own_bit(axis_name, bit):
    return (lax.axis_index(axis_name) >> bit) & 1


def ctx_bits(flip):
    bits = list(range(bit_count(lax.axis_size("ctx"))))
    return bits[::-1] if flip else bits


def scatter_sum(value, flip, with_fsdp=True):
    ctx_n = bit_count(lax.axis_size("ctx"))
    fsdp_n = bit_count(lax.axis_size("fsdp")) if with_fsdp else 0
    names = [("ctx", b) for b in range(ctx_n - 1, -1, -1)]
    names += [("fsdp", b) for b in range(fsdp_n - 1, -1, -1)]
    steps = [("fsdp", 0)] if with_fsdp else []
    steps += [("ctx", b) for b in ctx_bits(flip)]
    steps += [("fsdp", b) for b in range(1, fsdp_n)]
    rows = value.shape[0] >> len(names)
    value = value.reshape([2] * len(names) + [rows, value.shape[1]])
    for count, step in enumerate(steps):
        axis = names.index(step)
        names.pop(axis)
        mine = own_bit(*step)
        gone = lax.dynamic_index_in_dim(value, 1 - mine, axis, keepdims=False)
        kept = lax.dynamic_index_in_dim(value, mine, axis, keepdims=False)
        got = swap(gone.reshape(-1, gone.shape[-1]), *step).reshape(kept.shape)
        value = kept.astype(jnp.float32) + got.astype(jnp.float32)
        if count + 1 < len(steps):
            value = value.astype(jnp.bfloat16)
    return value


def gather_rows(shard, flip):
    ctx_size, fsdp_size = lax.axis_size("ctx"), lax.axis_size("fsdp")
    ctx_n, fsdp_n = bit_count(ctx_size), bit_count(fsdp_size)
    rows = shard.shape[0] // ctx_size
    cols = shard.shape[1]
    order = [("fsdp", b) for b in range(fsdp_n - 1, -1, -1)]
    order += [("ctx", b) for b in range(ctx_n - 1, -1, -1)]
    steps = [("fsdp", b) for b in range(fsdp_n - 1, 0, -1)]
    steps += [("ctx", b) for b in ctx_bits(flip)] + [("fsdp", 0)]
    value = lax.dynamic_slice_in_dim(shard, lax.axis_index("ctx") * rows, rows)
    names = []
    for step in steps:
        got = swap(value.reshape(-1, cols), *step).reshape(value.shape)
        low = own_bit(*step) == 0
        axis = sum(order.index(n) < order.index(step) for n in names)
        names.insert(axis, step)
        value = jnp.stack(
            [jnp.where(low, value, got), jnp.where(low, got, value)], axis=axis
        )
    return value.reshape(-1, cols)


def sum_all(value):
    for axis_name in ("fsdp", "ctx"):
        for bit in range(bit_count(lax.axis_size(axis_name))):
            value = value + swap(value, axis_name, bit)
    return value


def shards(
    tokens,
    cotangent,
    block_pair,
    segment_ids,
    attn_gain,
    query_gain,
    key_gain,
    ffn_gain,
    w_query,
    w_key,
    w_value,
    w_output,
    w_gate,
    w_up,
    w_down,
):
    ctx_count = lax.axis_size("ctx")
    ctx_rank = lax.axis_index("ctx")
    block_len = tokens.shape[3]
    model_width = tokens.shape[4]
    local_rows = 2 * block_len
    seq_rows = 2 * ctx_count * block_len
    group_size = Q_HEADS // KV_HEADS
    score_scale = HEAD_DIM ** (-0.5)
    blocks = jnp.stack([block_pair, 2 * ctx_count - 1 - block_pair], axis=1).reshape(-1)
    key_pos = (
        blocks[:, None] * block_len + jnp.arange(block_len, dtype=jnp.int32)[None, :]
    ).reshape(-1)
    key_seg = jnp.take(segment_ids.reshape(2 * ctx_count, block_len), blocks, axis=0).reshape(-1)
    own_pos = lax.dynamic_slice_in_dim(key_pos, ctx_rank * local_rows, local_rows)
    own_seg = lax.dynamic_slice_in_dim(key_seg, ctx_rank * local_rows, local_rows)
    cosine, sine_part = angles(own_pos, HEAD_DIM)
    inputs_now = tokens.reshape(local_rows, model_width).astype(jnp.float32)
    full_query, full_key, full_value, full_output, full_gate, full_up, full_down = (
        gather_rows(w_query, False),
        gather_rows(w_key, True),
        gather_rows(w_value, True),
        gather_rows(w_output, True),
        gather_rows(w_gate, False),
        gather_rows(w_up, True),
        None,
    )
    middle = w_down.shape[1] // 2
    full_down = jnp.concatenate(
        [gather_rows(w_down[:, :middle], False), gather_rows(w_down[:, middle:], True)], axis=1
    )
    attn_out, attn_normal, attn_factor = norm_parts(inputs_now, attn_gain)
    attn_in = attn_out.astype(jnp.bfloat16)
    query_raw = jnp.dot(attn_in, full_query, preferred_element_type=jnp.float32).reshape(
        local_rows, Q_HEADS, HEAD_DIM
    )
    key_raw = jnp.dot(attn_in, full_key, preferred_element_type=jnp.float32).reshape(
        local_rows, KV_HEADS, HEAD_DIM
    )
    value_low = jnp.dot(attn_in, full_value, preferred_element_type=jnp.float32).astype(
        jnp.bfloat16
    )
    query_gained, query_normal, query_factor = norm_parts(query_raw, query_gain)
    key_gained, key_normal, key_factor = norm_parts(key_raw, key_gain)
    query_low = (query_gained * cosine + turn_half(query_gained) * sine_part).astype(jnp.bfloat16)
    query_low = query_low.reshape(local_rows, KV_HEADS, group_size, HEAD_DIM)
    key_low = (key_gained * cosine + turn_half(key_gained) * sine_part).astype(jnp.bfloat16)
    key_low = key_low.reshape(local_rows, KV_HEADS * HEAD_DIM)

    def scores_for(key_block, first_key, block_size):
        block_pos = lax.dynamic_slice_in_dim(key_pos, first_key, block_size)
        block_seg = lax.dynamic_slice_in_dim(key_seg, first_key, block_size)
        allowed = (block_pos[None, :] <= own_pos[:, None]) & (
            block_seg[None, :] == own_seg[:, None]
        )
        raw_scores = (
            jnp.einsum(
                "qhgd,khd->qhgk",
                query_low,
                key_block.reshape(block_size, KV_HEADS, HEAD_DIM),
                preferred_element_type=jnp.float32,
            )
            * score_scale
        )
        allowed = allowed[:, None, None, :]
        return (jnp.where(allowed, raw_scores, MASKED_SCORE), allowed)

    start_state = (
        jnp.full((local_rows, KV_HEADS, group_size), MASKED_SCORE, jnp.float32),
        jnp.zeros((local_rows, KV_HEADS, group_size), jnp.float32),
        jnp.zeros((local_rows, KV_HEADS, group_size, HEAD_DIM), jnp.float32),
    )
    both_rows = lax.all_gather(
        jnp.concatenate([key_low, value_low], axis=1), "ctx", axis=0, tiled=True
    )
    key_rows, value_rows = jnp.split(both_rows, 2, axis=1)
    block_size = math.gcd(key_rows.shape[0], 256)

    def forward_advance(block_index, running_now):
        peak, denom_sum, weighted = running_now
        offset = block_index * block_size
        key_block = lax.dynamic_slice_in_dim(key_rows, offset, block_size)
        value_block = lax.dynamic_slice_in_dim(value_rows, offset, block_size).reshape(
            block_size, KV_HEADS, HEAD_DIM
        )
        masked, allowed = scores_for(key_block, offset, block_size)
        new_peak = jnp.maximum(peak, jnp.max(masked, axis=-1))
        attn_probs = jnp.where(allowed, jnp.exp(masked - new_peak[..., None]), 0.0)
        shrink = jnp.exp(peak - new_peak)
        denom_sum = denom_sum * shrink + jnp.sum(attn_probs, axis=-1)
        weighted = weighted * shrink[..., None] + jnp.einsum(
            "qhgk,khd->qhgd",
            attn_probs.astype(jnp.bfloat16),
            value_block,
            preferred_element_type=jnp.float32,
        )
        return (new_peak, denom_sum, weighted)

    peak, denom_sum, weighted = lax.fori_loop(
        0, key_rows.shape[0] // block_size, forward_advance, start_state
    )
    log_total = peak + jnp.log(denom_sum)
    attn_mix = weighted / denom_sum[..., None]
    mixed_low = attn_mix.reshape(local_rows, Q_HEADS * HEAD_DIM).astype(jnp.bfloat16)
    residual = inputs_now + jnp.dot(mixed_low, full_output, preferred_element_type=jnp.float32)
    ffn_out, ffn_normal, ffn_factor = norm_parts(residual, ffn_gain)
    ffn_in = ffn_out.astype(jnp.bfloat16)
    gate_value = jnp.dot(ffn_in, full_gate, preferred_element_type=jnp.float32)
    up_value = jnp.dot(ffn_in, full_up, preferred_element_type=jnp.float32)
    gate_sigmoid = jax.nn.sigmoid(gate_value)
    gate_silu = gate_value * gate_sigmoid
    activation = (gate_silu * up_value).astype(jnp.bfloat16)
    result = residual + jnp.dot(activation, full_down, preferred_element_type=jnp.float32)
    output = result.astype(jnp.bfloat16).reshape(tokens.shape)
    grad_low = cotangent.reshape(local_rows, model_width)
    down_wgrad = contract_rows(activation, grad_low).astype(jnp.bfloat16)
    act_grad = times_transposed(grad_low, full_down)
    gate_grad = (
        act_grad * up_value * gate_sigmoid * (1.0 + gate_value * (1.0 - gate_sigmoid))
    ).astype(jnp.bfloat16)
    up_grad = (act_grad * gate_silu).astype(jnp.bfloat16)
    gate_wgrad = contract_rows(ffn_in, gate_grad).astype(jnp.bfloat16)
    up_wgrad = contract_rows(ffn_in, up_grad).astype(jnp.bfloat16)
    ffn_in_grad = times_transposed(gate_grad, full_gate) + times_transposed(up_grad, full_up)
    ffn_back, ffn_gain_part = norm_back(ffn_in_grad, ffn_normal, ffn_factor, ffn_gain)
    ffn_gain_wgrad = jnp.sum(ffn_gain_part, axis=0)
    residual_grad = grad_low.astype(jnp.float32) + ffn_back
    gate_sum = scatter_sum(gate_wgrad, False)
    up_sum = scatter_sum(up_wgrad, True)
    down_sum = jnp.concatenate(
        [scatter_sum(down_wgrad[:, :middle], False), scatter_sum(down_wgrad[:, middle:], True)],
        axis=1,
    )
    residual_low = residual_grad.astype(jnp.bfloat16)
    output_wgrad = contract_rows(mixed_low, residual_low).astype(jnp.bfloat16)
    mixed_grad = times_transposed(residual_low, full_output).astype(jnp.bfloat16)
    mixed_grad = mixed_grad.reshape(local_rows, KV_HEADS, group_size, HEAD_DIM)
    row_delta = jnp.sum(mixed_grad.astype(jnp.float32) * attn_mix, axis=-1)
    back_state = (
        jnp.zeros((local_rows, KV_HEADS, group_size, HEAD_DIM), jnp.float32),
        jnp.zeros((seq_rows, KV_HEADS * HEAD_DIM), jnp.float32),
        jnp.zeros((seq_rows, KV_HEADS * HEAD_DIM), jnp.float32),
    )
    backward_key_rows, backward_value_rows = key_rows, value_rows
    backward_block_size = math.gcd(backward_key_rows.shape[0], 256)

    def backward_advance(block_index, running_now):
        query_grad, key_grad_all, value_grad_all = running_now
        offset = block_index * backward_block_size
        key_block = lax.dynamic_slice_in_dim(backward_key_rows, offset, backward_block_size)
        value_block = lax.dynamic_slice_in_dim(
            backward_value_rows, offset, backward_block_size
        ).reshape(backward_block_size, KV_HEADS, HEAD_DIM)
        masked, allowed = scores_for(key_block, offset, backward_block_size)
        attn_probs = jnp.where(allowed, jnp.exp(masked - log_total[..., None]), 0.0)
        value_part = jnp.einsum(
            "qhgk,qhgd->khd",
            attn_probs.astype(jnp.bfloat16),
            mixed_grad,
            preferred_element_type=jnp.float32,
        )
        prob_grad = jnp.einsum(
            "qhgd,khd->qhgk", mixed_grad, value_block, preferred_element_type=jnp.float32
        )
        score_grad = (attn_probs * (prob_grad - row_delta[..., None])).astype(jnp.bfloat16)
        query_grad = (
            query_grad
            + jnp.einsum(
                "qhgk,khd->qhgd",
                score_grad,
                key_block.reshape(backward_block_size, KV_HEADS, HEAD_DIM),
                preferred_element_type=jnp.float32,
            )
            * score_scale
        )
        key_part = (
            jnp.einsum("qhgk,qhgd->khd", score_grad, query_low, preferred_element_type=jnp.float32)
            * score_scale
        )
        key_grad_all = lax.dynamic_update_slice_in_dim(
            key_grad_all,
            lax.dynamic_slice_in_dim(key_grad_all, offset, backward_block_size)
            + key_part.reshape(backward_block_size, KV_HEADS * HEAD_DIM),
            offset,
            0,
        )
        value_grad_all = lax.dynamic_update_slice_in_dim(
            value_grad_all,
            lax.dynamic_slice_in_dim(value_grad_all, offset, backward_block_size)
            + value_part.reshape(backward_block_size, KV_HEADS * HEAD_DIM),
            offset,
            0,
        )
        return (query_grad, key_grad_all, value_grad_all)

    query_grad, key_grad_all, value_grad_all = lax.fori_loop(
        0, backward_key_rows.shape[0] // backward_block_size, backward_advance, back_state
    )
    key_grad = scatter_sum(key_grad_all.astype(jnp.bfloat16), False, False)
    value_grad = scatter_sum(value_grad_all.astype(jnp.bfloat16), True, False)
    key_grad = key_grad.reshape(local_rows, KV_HEADS, HEAD_DIM)
    key_turned = key_grad * cosine + turn_back(key_grad * sine_part)
    key_back, key_gain_part = norm_back(key_turned, key_normal, key_factor, key_gain)
    key_gain_local = jnp.sum(key_gain_part, axis=(0, 1))
    key_raw_grad = key_back.reshape(local_rows, KV_HEADS * HEAD_DIM).astype(jnp.bfloat16)
    query_grad = query_grad.reshape(local_rows, Q_HEADS, HEAD_DIM)
    query_turned = query_grad * cosine + turn_back(query_grad * sine_part)
    query_back, query_gain_part = norm_back(query_turned, query_normal, query_factor, query_gain)
    query_gain_local = jnp.sum(query_gain_part, axis=(0, 1))
    query_raw_grad = query_back.reshape(local_rows, Q_HEADS * HEAD_DIM).astype(jnp.bfloat16)
    value_raw_grad = value_grad.astype(jnp.bfloat16)
    query_wgrad = contract_rows(attn_in, query_raw_grad).astype(jnp.bfloat16)
    pair_wgrad = contract_rows(
        attn_in, jnp.concatenate([key_raw_grad, value_raw_grad], axis=1)
    ).astype(jnp.bfloat16)
    attn_in_grad = (
        times_transposed(query_raw_grad, full_query)
        + times_transposed(key_raw_grad, full_key)
        + times_transposed(value_raw_grad, full_value)
    )
    attn_back, attn_gain_part = norm_back(attn_in_grad, attn_normal, attn_factor, attn_gain)
    attn_gain_wgrad = jnp.sum(attn_gain_part, axis=0)
    input_grad = (residual_grad + attn_back).reshape(tokens.shape)
    query_sum = scatter_sum(query_wgrad, False)
    pair_sum = scatter_sum(pair_wgrad, True)
    key_sum, value_sum = jnp.split(pair_sum, 2, axis=1)
    output_sum = scatter_sum(output_wgrad, True)
    gains = sum_all(
        jnp.concatenate([attn_gain_wgrad, ffn_gain_wgrad, query_gain_local, key_gain_local])
    )
    share = model_width // (ctx_count * lax.axis_size("fsdp"))
    first = (ctx_rank * lax.axis_size("fsdp") + lax.axis_index("fsdp")) * share
    attn_gain_sum = lax.dynamic_slice_in_dim(gains, first, share)
    ffn_gain_sum = lax.dynamic_slice_in_dim(gains, model_width + first, share)
    query_gain_sum, key_gain_sum = jnp.split(gains[2 * model_width :], 2)
    return (
        output,
        input_grad,
        attn_gain_sum,
        query_gain_sum,
        key_gain_sum,
        ffn_gain_sum,
        query_sum,
        key_sum,
        value_sum,
        output_sum,
        gate_sum,
        up_sum,
        down_sum,
    )


def solution(mesh):
    placed = (
        P("fsdp", "ctx", None, None, None),
        P("fsdp", "ctx", None, None, None),
        P(),
        P("fsdp", None),
        P(),
        P(),
        P(),
        P(),
        P("fsdp", None),
        P("fsdp", None),
        P("fsdp", None),
        P("fsdp", None),
        P("fsdp", None),
        P("fsdp", None),
        P("fsdp", None),
    )
    return jax.shard_map(
        shards,
        mesh=mesh,
        in_specs=placed,
        out_specs=(
            P("fsdp", "ctx", None, None, None),
            P("fsdp", "ctx", None, None, None),
            P(("ctx", "fsdp")),
            P(),
            P(),
            P(("ctx", "fsdp")),
            P(("ctx", "fsdp"), None),
            P(("ctx", "fsdp"), None),
            P(("ctx", "fsdp"), None),
            P(("ctx", "fsdp"), None),
            P(("ctx", "fsdp"), None),
            P(("ctx", "fsdp"), None),
            P(("ctx", "fsdp"), None),
        ),
        check_vma=False,
    )
```
